32 devices in a mesh: groups: 2 (over y), box: 4 (over z), dir: 2 (over x), sub: 2 (over core).
Axes of the slice: x: 2, y: 2, z: 4, core: 2. Of those that a mesh axis runs over, the one named last changes fastest.
Arguments:
- history_currents: bfloat16 [128, 16, 128], P(('groups', 'box')), parts along dimension 0, may hold values from -6 to 6
- history_rays: bfloat16 [128, 16, 10240], P(('groups', 'box'), None, ('dir', 'sub')), parts along dimension 0, may hold values from -6 to 6
- incident: float32 [128, 4, 128], P(('groups', 'box')), parts along dimension 0, may hold values from -6 to 6
- near_blocks: bfloat16 [64, 12, 4, 128, 128], P('box', None, ('dir', 'sub')), may hold values from -0.0546875 to 0.0546875
- near_partners: int32 [64, 12], P('box'), may hold values from 0 to 63, as said below
- self_inverse: float32 [64, 128, 128], P('box'), may hold values from -0.5 to 0.5
- projection: bfloat16 [128, 10240], P(None, ('dir', 'sub')), may hold values from -0.5 to 0.5
- reception: bfloat16 [10240, 128], P(('dir', 'sub')), may hold values from -0.03125 to 0.03125
- translations: bfloat16 [316, 10240], P(None, ('dir', 'sub')), may hold values from -6 to 6
- send_source: int32 [4, 4, 8], P('box'), may hold values from 0 to 15
- send_delay: int32 [4, 4, 8], P('box'), may hold values from 1 to 16
- send_target: int32 [4, 4, 8], P('box'), may hold values from 0 to 15
- send_class: int32 [4, 4, 8], P('box'), may hold values from 0 to 315
- slot_counts: int32 [4, 4], P('box'), may hold values from 0 to 8, as said below
Outputs:
- currents: bfloat16 [128, 4, 128], P(('groups', 'box')), parts along dimension 0
- rays: bfloat16 [128, 4, 10240], P(('groups', 'box'), None, ('dir', 'sub')), parts along dimension 0
The draws below stay inside these ranges and needn't reach their ends.
There are 2 independent parts, one for each index of `groups`. The reference program is written for one: setup_inputs(seed, part) draws one part's arguments, and reference() takes and returns one part's arrays. A program takes and returns all parts, laid end to end along the dimension named above; an argument that names none is the same for every part. Nothing has to cross between parts.
Inputs may be any that keep to these rules, and one draw needn't show every extreme that they name: |near_partners[b, n] - b| <= 16; near_partners[b, 0] = b. `slot_counts`: every sender has 8 live slots to some receiver, and some receiver has 8 live slots from every sender.
All inputs are finite; a program needn't handle non-finite values.
Results may differ from the reference program's by a relative error of at most 0.0054.
Values may be sent and summed in bfloat16 or wider, within the bound.
A program may use at most 64 MiB of HBM per device.

```python
import jax
import jax.numpy as jnp
from jax import lax

S = 128
K = 10240
NTRANS = 316
NEAR = 12
H = 16
NT = 4
CAP = 8
B_DEV = 16
L = 4
NB = 64
N_BOX = 4


def draw_near_partners(key, part):
    key = jax.random.fold_in(key, 11)
    box_total = B_DEV * N_BOX
    offsets = jax.random.randint(key, (box_total, NEAR), -B_DEV, B_DEV + 1)
    column = jnp.arange(NEAR)[None, :]
    offsets = jnp.where(column == 0, 0, jnp.where(column == 1, -B_DEV, jnp.where(column == 2, B_DEV, offsets)))
    boxes = jnp.arange(box_total)[:, None]
    return jnp.clip(boxes + offsets, 0, box_total - 1).astype(jnp.int32)


def draw_send_source(key, part):
    key = jax.random.fold_in(key, 12)
    return jax.random.randint(key, (N_BOX, N_BOX, CAP), 0, B_DEV).astype(jnp.int32)


def draw_send_delay(key, part):
    key = jax.random.fold_in(key, 13)
    values = jax.random.randint(key, (N_BOX, N_BOX, CAP), 1, H + 1)
    flat = jnp.arange(N_BOX * N_BOX * CAP).reshape(N_BOX, N_BOX, CAP)
    values = jnp.where(flat == 0, H, jnp.where(flat == 1, 1, values))
    return values.astype(jnp.int32)


def draw_send_target(key, part):
    key = jax.random.fold_in(key, 14)
    return jax.random.randint(key, (N_BOX, N_BOX, CAP), 0, B_DEV).astype(jnp.int32)


def draw_send_class(key, part):
    key = jax.random.fold_in(key, 15)
    return jax.random.randint(key, (N_BOX, N_BOX, CAP), 0, NTRANS).astype(jnp.int32)


def draw_slot_counts(key, part):
    key = jax.random.fold_in(key, 16)
    first, second, third = jax.random.split(key, 3)
    base = jax.random.randint(first, (N_BOX, N_BOX), 0, CAP + 1)
    chosen = jax.random.randint(second, (N_BOX,), 0, N_BOX)
    column = jnp.arange(N_BOX)[None, :]
    base = jnp.where(column == chosen[:, None], CAP, base)
    full_column = jax.random.randint(third, (), 0, N_BOX)
    base = jnp.where(column == full_column, CAP, base)
    return base.astype(jnp.int32)


def levels(key, shape, cuts, low, high):
    level = 1.0
    for axis_at, blocks in cuts:
        steps = jax.random.uniform(jax.random.fold_in(jax.random.fold_in(key, 6), axis_at), (blocks,), jnp.float32, low / len(cuts), high / len(cuts))
        level = level * jnp.repeat(jnp.exp(steps), shape[axis_at] // blocks).reshape((-1,) + (1,) * (len(shape) - 1 - axis_at))
    return level


def centred(rng, shape, deviation, most, cuts=(), held_as=jnp.bfloat16):
    entries = deviation * jax.random.normal(rng, shape, jnp.float32)
    if cuts:
        entries = entries * levels(rng, shape, cuts, -0.22, 0.18)
    return jnp.clip(entries, -most, most).astype(held_as)


def setup_inputs(seed: int = 0, part: int = 0) -> dict:
    keys = jax.random.split(jax.random.key(seed), 15)
    own_keys = jax.random.split(jax.random.fold_in(keys[14], part), 15)
    history_currents = centred(own_keys[0], (NB, H, S), 1.0, 6.0, ((0, 4),))
    history_rays = centred(own_keys[1], (NB, H, K), 1.0, 6.0, ((0, 4), (2, 4)))
    incident = centred(own_keys[2], (NB, NT, S), 1.0, 6.0, ((0, 4),), jnp.float32)
    near_blocks = centred(keys[3], (NB, NEAR, L, S, S), (2 * NEAR * L * S) ** -0.5, 0.0546875, ((0, 4), (2, 4)))
    near_partners = draw_near_partners(jax.random.fold_in(keys[14], 71), part)
    self_inverse = centred(keys[5], (NB, S, S), S ** -0.5, 0.5, ((0, 4),), jnp.float32)
    projection = centred(keys[6], (S, K), S ** -0.5, 0.5, ((1, 4),))
    reception = centred(keys[7], (K, S), (4 * K) ** -0.5, 0.03125, ((0, 4),))
    translations = centred(keys[8], (NTRANS, K), 1.0, 6.0, ((1, 4),))
    send_source = draw_send_source(jax.random.fold_in(keys[14], 71), part)
    send_delay = draw_send_delay(jax.random.fold_in(keys[14], 71), part)
    send_target = draw_send_target(jax.random.fold_in(keys[14], 71), part)
    send_class = draw_send_class(jax.random.fold_in(keys[14], 71), part)
    slot_counts = draw_slot_counts(jax.random.fold_in(keys[14], 71), part)
    return dict(history_currents=history_currents, history_rays=history_rays, incident=incident, near_blocks=near_blocks, near_partners=near_partners, self_inverse=self_inverse, projection=projection, reception=reception, translations=translations, send_source=send_source, send_delay=send_delay, send_target=send_target, send_class=send_class, slot_counts=slot_counts)


def near_box(pieces):
    blocks, partner_hist = pieces
    return jnp.einsum('nlst,nlt->s', blocks.astype(jnp.float32), partner_hist.astype(jnp.float32))


def reference(history_currents, history_rays, incident, near_blocks, near_partners, self_inverse, projection, reception, translations, send_source, send_delay, send_target, send_class, slot_counts):
    box_total = B_DEV * N_BOX
    lag_span = near_blocks.shape[2]
    size_s = history_currents.shape[2]
    size_k = history_rays.shape[2]
    cur_buf = jnp.concatenate([history_currents, jnp.zeros((box_total, NT, size_s), jnp.bfloat16)], axis=1)
    ray_buf = jnp.concatenate([history_rays, jnp.zeros((box_total, NT, size_k), jnp.bfloat16)], axis=1)
    sender = jnp.arange(N_BOX, dtype=jnp.int32)[:, None, None]
    receiver = jnp.arange(N_BOX, dtype=jnp.int32)[None, :, None]
    slot_index = jnp.arange(CAP, dtype=jnp.int32)[None, None, :]
    source_global = (sender * B_DEV + send_source).reshape(-1).astype(jnp.int32)
    target_global = (receiver * B_DEV + send_target).reshape(-1).astype(jnp.int32)
    live_slots = (slot_index < slot_counts[:, :, None]).reshape(-1)
    class_ids = send_class.reshape(-1).astype(jnp.int32)
    delay_ids = send_delay.reshape(-1).astype(jnp.int32)
    trans_table = translations.astype(jnp.float32)
    for moment in range(NT):
        frames = cur_buf[:, H + moment - lag_span:H + moment][:, ::-1]
        partner_hist = frames[near_partners]
        near_field = lax.map(near_box, (near_blocks, partner_hist))
        slot_rows = ray_buf[source_global, (H + moment - delay_ids).astype(jnp.int32)]
        slot_terms = slot_rows.astype(jnp.float32) * trans_table[class_ids]
        slot_terms = jnp.where(live_slots[:, None], slot_terms, jnp.float32(0.0))
        incoming = jax.ops.segment_sum(slot_terms, target_global, num_segments=box_total)
        far_field = jnp.dot(incoming.astype(jnp.bfloat16), reception, preferred_element_type=jnp.float32)
        total_field = near_field + far_field
        current = jnp.einsum('bst,bt->bs', self_inverse, incident[:, moment] - total_field, precision=lax.Precision.HIGHEST)
        current_low = current.astype(jnp.bfloat16)
        new_rays = jnp.dot(current_low, projection, preferred_element_type=jnp.float32).astype(jnp.bfloat16)
        cur_buf = cur_buf.at[:, H + moment].set(current_low)
        ray_buf = ray_buf.at[:, H + moment].set(new_rays)
    return cur_buf[:, H:], ray_buf[:, H:]
```

```python
import functools

import jax
import jax.numpy as jnp
from jax import lax
from jax.experimental import pallas as pl
from jax.experimental.pallas import tpu as pltpu
from jax.sharding import PartitionSpec as P

MESH = pl.DeviceIdType.MESH
NT_DIMS = (((1,), (1,)), ((), ()))
F32 = jnp.float32
BF16 = jnp.bfloat16


def march(
    peers,
    dirs,
    subs,
    hist_cur,
    hist_rays,
    incident,
    near_hbm,
    near_pick,
    inverse_hbm,
    projection,
    reception,
    translations,
    class_pick,
    hist_pick,
    new_pick,
    target_pick,
    out,
    near_v,
    inverse_v,
    inverse_cat,
    win,
    cur_all,
    factors,
    hist_terms,
    far_send,
    far_recv,
    part,
    near_sem,
    inverse_sem,
    win_send_sem,
    win_recv_sem,
    far_send_sem,
    far_recv_sem,
    part_send_sem,
    part_recv_sem,
):
    steps, boxes, width = incident.shape
    lag_span = hist_cur.shape[0]
    lags = near_v.shape[2]
    near = near_v.shape[1]
    rays = projection.shape[1]
    slots = class_pick.shape[0]
    spread = dirs * subs
    box = lax.axis_index("box")
    piece = lax.axis_index("dir") * subs + lax.axis_index("sub")
    chunk = 512 if rays % 512 == 0 else (256 if rays % 256 == 0 else 128)

    near_copy = pltpu.make_async_copy(near_hbm, near_v, near_sem)
    inverse_copy = pltpu.make_async_copy(inverse_hbm, inverse_v, inverse_sem)
    inverse_copy.start()
    near_copy.start()

    def peer_of(offset):
        return {"box": lax.rem(box + offset, peers)}

    def sibling_of(offset):
        other = lax.rem(piece + offset, spread)
        return {"dir": other // subs, "sub": lax.rem(other, subs)}

    win[1, pl.ds(0, lag_span)] = hist_cur[...]
    win[0] = jnp.zeros(win.shape[1:], F32)
    win[2] = jnp.zeros(win.shape[1:], F32)
    cur_all[...] = jnp.zeros(cur_all.shape, BF16)

    barrier = pltpu.get_barrier_semaphore()
    for offset in range(1, peers):
        pl.semaphore_signal(barrier, inc=1, device_id=peer_of(offset), device_id_type=MESH)
    for offset in range(1, spread):
        pl.semaphore_signal(barrier, inc=1, device_id=sibling_of(offset), device_id_type=MESH)

    pl.semaphore_wait(barrier, peers - 1 + spread - 1)

    def window_copy(order, side):
        span = pl.ds(0, lag_span) if order == 0 else pl.ds(lag_span + order - 1, 1)
        offset = 1 if side == 0 else peers - 1
        return pltpu.make_async_remote_copy(
            src_ref=win.at[1, span],
            dst_ref=win.at[0 if side == 0 else 2, span],
            send_sem=win_send_sem.at[order, side],
            recv_sem=win_recv_sem.at[order, side],
            device_id=peer_of(offset),
            device_id_type=MESH,
        )

    has_next = box < peers - 1
    has_prev = box > 0

    def start_window(order):
        @pl.when(has_next)
        def _():
            window_copy(order, 0).start()

        @pl.when(has_prev)
        def _():
            window_copy(order, 1).start()

    def wait_window(order):
        @pl.when(has_prev)
        def _():
            window_copy(order, 0).wait_recv()

        @pl.when(has_next)
        def _():
            window_copy(order, 1).wait_recv()

    def wait_window_sent(order):
        @pl.when(has_next)
        def _():
            window_copy(order, 0).wait_send()

        @pl.when(has_prev)
        def _():
            window_copy(order, 1).wait_send()

    start_window(0)

    def far_copy(step, offset):
        return pltpu.make_async_remote_copy(
            src_ref=far_send.at[step, lax.rem(box + offset, peers)],
            dst_ref=far_recv.at[step, offset],
            send_sem=far_send_sem.at[step, offset],
            recv_sem=far_recv_sem.at[step, offset],
            device_id=peer_of(offset),
            device_id_type=MESH,
        )

    def part_copy(step, offset):
        return pltpu.make_async_remote_copy(
            src_ref=part.at[step, piece],
            dst_ref=part.at[step, piece],
            send_sem=part_send_sem.at[step, offset],
            recv_sem=part_recv_sem.at[step, offset],
            device_id=sibling_of(offset),
            device_id_type=MESH,
        )

    def columns(index):
        return pl.ds(pl.multiple_of(index * chunk, chunk), chunk)

    def history_part(index, total):
        at = columns(index)
        factor = jnp.dot(class_pick[...], translations[:, at], preferred_element_type=F32).astype(BF16)
        factors[:, at] = factor
        picked = jnp.dot(hist_pick[...], hist_rays[:, at], preferred_element_type=F32).astype(BF16)
        terms = jnp.concatenate(
            [picked[t * slots : (t + 1) * slots] * factor for t in range(steps)], axis=0
        )
        return total + jnp.dot(terms, reception[at, :], preferred_element_type=F32)

    hist_terms[...] = lax.fori_loop(
        0, rays // chunk, history_part, jnp.zeros((steps * slots, width), F32)
    )

    def send_far(step):
        terms = hist_terms[pl.ds(step * slots, slots), :]
        if step > 0:
            picked = jnp.dot(
                new_pick[pl.ds(step * slots, slots), :], cur_all[...], preferred_element_type=F32
            ).astype(BF16)

            def new_part(index, total):
                at = columns(index)
                ray = jnp.dot(picked, projection[:, at], preferred_element_type=F32).astype(BF16)
                return total + jnp.dot(
                    ray * factors[:, at], reception[at, :], preferred_element_type=F32
                )

            terms = lax.fori_loop(0, rays // chunk, new_part, terms)
        far = jnp.dot(
            target_pick[...], terms, precision=lax.Precision.HIGHEST, preferred_element_type=F32
        )
        far_send[step] = far.reshape(peers, boxes, width)
        for offset in range(1, peers):
            far_copy(step, offset).start()

    row = lax.broadcasted_iota(jnp.int32, (boxes, width), 0)

    for step in range(steps):
        send_far(step)
        if step == 0:
            inverse_copy.wait()

            def split(index, carry):
                whole = inverse_v[index]
                high = whole.astype(BF16)
                low = (whole - high.astype(F32)).astype(BF16)
                inverse_cat[index] = jnp.concatenate([high, low], axis=1)
                return carry

            lax.fori_loop(0, boxes, split, 0)
            near_copy.wait()
        wait_window(step)

        pieces = []
        for lag in range(lags):
            at = lag_span + step - (piece * lags + lag + 1)
            table = jnp.concatenate([win[0, at], win[1, at], win[2, at]], axis=0).astype(BF16)
            gathered = jnp.dot(near_pick[...], table, preferred_element_type=F32).astype(BF16)
            for n in range(near):
                pieces.append(gathered[n * boxes : (n + 1) * boxes])
        sources = jnp.concatenate(pieces, axis=1)

        def near_part(index, total):
            blocks = jnp.concatenate(
                [near_v[index, n, lag] for lag in range(lags) for n in range(near)], axis=1
            )
            value = lax.dot_general(sources, blocks, NT_DIMS, preferred_element_type=F32)
            return total + jnp.where(row == index, value, 0.0)

        field = lax.fori_loop(0, boxes, near_part, jnp.zeros((boxes, width), F32))
        field = field + far_send[step, box]
        for offset in range(1, peers):
            far_copy(step, offset).wait_recv()
            field = field + far_recv[step, offset]
        part[step, piece] = field
        for offset in range(1, spread):
            part_copy(step, offset).start()
        for offset in range(1, spread):
            part_copy(step, offset).wait_recv()
        total = part[step, 0]
        for other in range(1, spread):
            total = total + part[step, other]

        drive = incident[step] - total
        high = drive.astype(BF16)
        low = (drive - high.astype(F32)).astype(BF16)
        left = jnp.concatenate(
            [
                jnp.concatenate([high, high], axis=1),
                jnp.concatenate([low, jnp.zeros_like(low)], axis=1),
            ],
            axis=0,
        )

        def solve_part(index, total):
            value = lax.dot_general(left, inverse_cat[index], NT_DIMS, preferred_element_type=F32)
            return total + jnp.where(row == index, value[:boxes] + value[boxes:], 0.0)

        current = lax.fori_loop(0, boxes, solve_part, jnp.zeros((boxes, width), F32)).astype(BF16)
        out[step] = current
        if step < steps - 1:
            cur_all[pl.ds(step * boxes, boxes), :] = current
            win[1, lag_span + step] = current.astype(F32)
            start_window(step + 1)

    for step in range(steps):
        wait_window_sent(step)
        for offset in range(1, peers):
            far_copy(step, offset).wait_send()
        for offset in range(1, spread):
            part_copy(step, offset).wait_send()


def body(
    history_currents,
    history_rays,
    incident,
    near_blocks,
    near_partners,
    self_inverse,
    projection,
    reception,
    translations,
    send_source,
    send_delay,
    send_target,
    send_class,
    slot_counts,
):
    boxes, hist_len, width = history_currents.shape
    rays = history_rays.shape[2]
    steps = incident.shape[1]
    near, lags = near_blocks.shape[1:3]
    peers, dirs, subs = (lax.axis_size(a) for a in ("box", "dir", "sub"))
    spread = dirs * subs
    lag_span = lags * spread
    box = lax.axis_index("box")
    capacity = send_source.shape[2]
    slots = peers * capacity
    classes = translations.shape[0]

    source = send_source.reshape(slots)
    delay = send_delay.reshape(slots)
    class_ids = send_class.reshape(slots)
    moment = jnp.arange(steps)[:, None]
    back = moment - delay[None, :]
    hist_row = jnp.where(back < 0, source * hist_len + hist_len + back, -1).reshape(-1, 1)
    new_row = jnp.where(back >= 0, back * boxes + source, -1).reshape(-1, 1)
    hist_pick = (hist_row == jnp.arange(boxes * hist_len)).astype(BF16)
    new_pick = (new_row == jnp.arange(steps * boxes)).astype(BF16)
    class_pick = (class_ids[:, None] == jnp.arange(classes)).astype(BF16)
    live = jnp.arange(capacity)[None, :] < slot_counts[0][:, None]
    dest = jnp.where(live, jnp.arange(peers)[:, None] * boxes + send_target[0], -1).reshape(1, slots)
    target_pick = (jnp.arange(peers * boxes)[:, None] == dest).astype(F32)
    local = (near_partners - (box - 1) * boxes).T.reshape(-1, 1)
    near_pick = (local == jnp.arange(3 * boxes)).astype(BF16)
    hist_cur = history_currents[:, hist_len - lag_span :].transpose(1, 0, 2).astype(F32)

    vmem = pl.BlockSpec(memory_space=pltpu.VMEM)
    hbm = pl.BlockSpec(memory_space=pl.ANY)
    dma = pltpu.SemaphoreType.DMA
    currents = pl.pallas_call(
        functools.partial(march, peers, dirs, subs),
        out_shape=jax.ShapeDtypeStruct((steps, boxes, width), BF16),
        in_specs=[vmem, vmem, vmem, hbm, vmem, hbm, vmem, vmem, vmem, vmem, vmem, vmem, vmem],
        out_specs=vmem,
        scratch_shapes=[
            pltpu.VMEM(near_blocks.shape, BF16),
            pltpu.VMEM(self_inverse.shape, F32),
            pltpu.VMEM((boxes, width, 2 * width), BF16),
            pltpu.VMEM((3, lag_span + steps, boxes, width), F32),
            pltpu.VMEM((steps * boxes, width), BF16),
            pltpu.VMEM((slots, rays), BF16),
            pltpu.VMEM((steps * slots, width), F32),
            pltpu.VMEM((steps, peers, boxes, width), F32),
            pltpu.VMEM((steps, peers, boxes, width), F32),
            pltpu.VMEM((steps, spread, boxes, width), F32),
            dma,
            dma,
            dma((steps, 2)),
            dma((steps, 2)),
            dma((steps, peers)),
            dma((steps, peers)),
            dma((steps, spread)),
            dma((steps, spread)),
        ],
        compiler_params=pltpu.CompilerParams(
            collective_id=0, has_side_effects=True, vmem_limit_bytes=48 * 1024 * 1024
        ),
    )(
        hist_cur,
        history_rays.reshape(boxes * hist_len, rays),
        incident.transpose(1, 0, 2),
        near_blocks,
        near_pick,
        self_inverse,
        projection,
        reception,
        translations,
        class_pick,
        hist_pick,
        new_pick,
        target_pick,
    )
    currents = currents.transpose(1, 0, 2)
    new_rays = jnp.einsum("bts,sk->btk", currents, projection, preferred_element_type=F32)
    return currents, new_rays.astype(BF16)


def solution(mesh):
    return jax.shard_map(
        body,
        mesh=mesh,
        in_specs=(
            P(("groups", "box"), None, None),
            P(("groups", "box"), None, ("dir", "sub")),
            P(("groups", "box"), None, None),
            P("box", None, ("dir", "sub"), None, None),
            P("box", None),
            P("box", None, None),
            P(None, ("dir", "sub")),
            P(("dir", "sub"), None),
            P(None, ("dir", "sub")),
            P("box", None, None),
            P("box", None, None),
            P("box", None, None),
            P("box", None, None),
            P("box", None),
        ),
        out_specs=(P(("groups", "box"), None, None), P(("groups", "box"), None, ("dir", "sub"))),
        check_vma=False,
    )
```

```python
import functools

import jax
import jax.numpy as jnp
from jax import lax
from jax.experimental import pallas as pl
from jax.experimental.pallas import tpu as pltpu
from jax.sharding import PartitionSpec as P

MESH = pl.DeviceIdType.MESH
NT_DIMS = (((1,), (1,)), ((), ()))
F32 = jnp.float32
BF16 = jnp.bfloat16


def march(
    peers,
    dirs,
    subs,
    source_ids,
    delay_ids,
    target_ids,
    class_ids,
    live_counts,
    partner_ids,
    hist_cur,
    incident,
    rays_hbm,
    near_hbm,
    inverse_hbm,
    projection_hbm,
    reception_hbm,
    translations_hbm,
    out,
    hist_rays,
    near_v,
    inverse_v,
    projection,
    reception,
    translations,
    inverse_cat,
    hist_f32,
    win,
    cur_all,
    near_pick,
    new_pick,
    target_pick,
    factors,
    hist_terms,
    far_send,
    far_recv,
    part,
    copy_sems,
    win_send_sem,
    win_recv_sem,
    far_send_sem,
    far_recv_sem,
    part_send_sem,
    part_recv_sem,
):
    boxes, steps, width = incident.shape
    hist_len = hist_cur.shape[1]
    lags = near_v.shape[2]
    near = near_v.shape[1]
    rays = projection.shape[1]
    capacity = source_ids.shape[2]
    slots = peers * capacity
    spread = dirs * subs
    lag_span = lags * spread
    box = lax.axis_index("box")
    piece = lax.axis_index("dir") * subs + lax.axis_index("sub")
    chunk = 512 if rays % 512 == 0 else (256 if rays % 256 == 0 else 128)

    copies = [
        pltpu.make_async_copy(src, dst, copy_sems.at[i])
        for i, (src, dst) in enumerate(
            (
                (translations_hbm, translations),
                (rays_hbm, hist_rays),
                (reception_hbm, reception),
                (inverse_hbm, inverse_v),
                (near_hbm, near_v),
                (projection_hbm, projection),
            )
        )
    ]
    for copy in copies:
        copy.start()

    def peer_of(offset):
        return {"box": lax.rem(box + offset, peers)}

    def sibling_of(offset):
        other = lax.rem(piece + offset, spread)
        return {"dir": other // subs, "sub": lax.rem(other, subs)}

    hist_f32[...] = hist_cur[...].astype(F32)
    for back in range(lag_span):
        win[1, back] = hist_f32[:, hist_len - lag_span + back, :]
    win[0] = jnp.zeros(win.shape[1:], F32)
    win[2] = jnp.zeros(win.shape[1:], F32)
    cur_all[...] = jnp.zeros(cur_all.shape, BF16)

    barrier = pltpu.get_barrier_semaphore()
    for offset in range(1, peers):
        pl.semaphore_signal(barrier, inc=1, device_id=peer_of(offset), device_id_type=MESH)
    for offset in range(1, spread):
        pl.semaphore_signal(barrier, inc=1, device_id=sibling_of(offset), device_id_type=MESH)


    def column_of(count, value):
        tiles = []
        rows = lax.broadcasted_iota(jnp.int32, (8, 1), 0)
        for start in range(0, count, 8):
            tile = jnp.full((8, 1), -1, jnp.int32)
            for i in range(min(8, count - start)):
                tile = jnp.where(rows == i, value(start + i), tile)
            tiles.append(tile)
        return jnp.concatenate(tiles, axis=0)[:count]

    def pick(ids, size):
        lanes = lax.broadcasted_iota(jnp.int32, (ids.shape[0], size), 1)
        return jnp.where(lanes == ids, 1.0, 0.0)

    def slot_of(ref):
        return column_of(slots, lambda j: ref[0, j // capacity, j % capacity])

    source, delay = slot_of(source_ids), slot_of(delay_ids)
    hist_rows = []
    new_rows = []
    for step in range(steps):
        back = step - delay
        hist_rows.append(jnp.where(back < 0, source * hist_len + hist_len + back, -1))
        new_rows.append(jnp.where(back >= 0, back * boxes + source, -1))
    hist_pick = pick(jnp.concatenate(hist_rows, axis=0), boxes * hist_len).astype(BF16)
    new_pick[...] = pick(jnp.concatenate(new_rows, axis=0), steps * boxes).astype(BF16)
    class_pick = pick(slot_of(class_ids), translations.shape[0]).astype(BF16)
    live = column_of(slots, lambda j: live_counts[0, j // capacity])
    place = lax.broadcasted_iota(jnp.int32, (slots, 1), 0)
    dest = jnp.where(place % capacity < live, place // capacity * boxes + slot_of(target_ids), -1)
    target_pick[...] = pick(dest, peers * boxes)
    partner = column_of(near * boxes, lambda j: partner_ids[j % boxes, j // boxes])
    near_pick[...] = pick(partner - (box - 1) * boxes, 3 * boxes).astype(BF16)
    pl.semaphore_wait(barrier, peers - 1 + spread - 1)

    def window_copy(order, side):
        span = pl.ds(0, lag_span) if order == 0 else pl.ds(lag_span + order - 1, 1)
        offset = 1 if side == 0 else peers - 1
        return pltpu.make_async_remote_copy(
            src_ref=win.at[1, span],
            dst_ref=win.at[0 if side == 0 else 2, span],
            send_sem=win_send_sem.at[order, side],
            recv_sem=win_recv_sem.at[order, side],
            device_id=peer_of(offset),
            device_id_type=MESH,
        )

    has_next = box < peers - 1
    has_prev = box > 0

    def start_window(order):
        @pl.when(has_next)
        def _():
            window_copy(order, 0).start()

        @pl.when(has_prev)
        def _():
            window_copy(order, 1).start()

    def wait_window(order):
        @pl.when(has_prev)
        def _():
            window_copy(order, 0).wait_recv()

        @pl.when(has_next)
        def _():
            window_copy(order, 1).wait_recv()

    def wait_window_sent(order):
        @pl.when(has_next)
        def _():
            window_copy(order, 0).wait_send()

        @pl.when(has_prev)
        def _():
            window_copy(order, 1).wait_send()

    start_window(0)

    def far_copy(step, offset):
        return pltpu.make_async_remote_copy(
            src_ref=far_send.at[step, lax.rem(box + offset, peers)],
            dst_ref=far_recv.at[step, offset],
            send_sem=far_send_sem.at[step, offset],
            recv_sem=far_recv_sem.at[step, offset],
            device_id=peer_of(offset),
            device_id_type=MESH,
        )

    def part_copy(step, offset):
        return pltpu.make_async_remote_copy(
            src_ref=part.at[step, piece],
            dst_ref=part.at[step, piece],
            send_sem=part_send_sem.at[step, offset],
            recv_sem=part_recv_sem.at[step, offset],
            device_id=sibling_of(offset),
            device_id_type=MESH,
        )

    def columns(index):
        return pl.ds(index * chunk, chunk)

    def history_part(index, total):
        at = columns(index)
        factor = jnp.dot(class_pick, translations[:, at], preferred_element_type=F32).astype(BF16)
        factors[:, at] = factor
        picked = jnp.dot(hist_pick, hist_rays[:, at], preferred_element_type=F32).astype(BF16)
        terms = jnp.concatenate(
            [picked[t * slots : (t + 1) * slots] * factor for t in range(steps)], axis=0
        )
        return total + jnp.dot(terms, reception[at, :], preferred_element_type=F32)

    for copy in copies[:3]:
        copy.wait()
    total = jnp.zeros((steps * slots, width), F32)
    for index in range(rays // chunk):
        total = history_part(index, total)
    hist_terms[...] = total

    def send_far(step):
        terms = hist_terms[pl.ds(step * slots, slots), :]
        if step > 0:
            picked = jnp.dot(
                new_pick[pl.ds(step * slots, slots), :], cur_all[...], preferred_element_type=F32
            ).astype(BF16)

            def new_part(index, total):
                at = columns(index)
                ray = jnp.dot(picked, projection[:, at], preferred_element_type=F32).astype(BF16)
                return total + jnp.dot(
                    ray * factors[:, at], reception[at, :], preferred_element_type=F32
                )

            for index in range(rays // chunk):
                terms = new_part(index, terms)
        far = lax.dot_general(
            target_pick[...],
            terms,
            (((0,), (0,)), ((), ())),
            precision=lax.Precision.HIGHEST,
            preferred_element_type=F32,
        )
        far_send[step] = far.reshape(peers, boxes, width)
        for offset in range(1, peers):
            far_copy(step, offset).start()

    row = lax.broadcasted_iota(jnp.int32, (boxes, width), 0)

    for step in range(steps):
        send_far(step)
        if step == 0:
            copies[3].wait()

            def split(index, carry):
                whole = inverse_v[index]
                high = whole.astype(BF16)
                low = (whole - high.astype(F32)).astype(BF16)
                inverse_cat[index] = jnp.concatenate([high, low], axis=1)
                return carry

            lax.fori_loop(0, boxes, split, 0)
            copies[4].wait()
            copies[5].wait()
        wait_window(step)

        pieces = []
        for lag in range(lags):
            at = lag_span + step - (piece * lags + lag + 1)
            table = jnp.concatenate([win[0, at], win[1, at], win[2, at]], axis=0).astype(BF16)
            gathered = jnp.dot(near_pick[...], table, preferred_element_type=F32).astype(BF16)
            for n in range(near):
                pieces.append(gathered[n * boxes : (n + 1) * boxes])
        sources = jnp.concatenate(pieces, axis=1)

        def near_part(index, total):
            blocks = jnp.concatenate(
                [near_v[index, n, lag] for lag in range(lags) for n in range(near)], axis=1
            )
            value = lax.dot_general(sources, blocks, NT_DIMS, preferred_element_type=F32)
            return total + jnp.where(row == index, value, 0.0)

        field = jnp.zeros((boxes, width), F32)
        for index in range(boxes):
            field = near_part(index, field)
        field = field + far_send[step, box]
        for offset in range(1, peers):
            far_copy(step, offset).wait_recv()
            field = field + far_recv[step, offset]
        part[step, piece] = field
        for offset in range(1, spread):
            part_copy(step, offset).start()
        for offset in range(1, spread):
            part_copy(step, offset).wait_recv()
        total = part[step, 0]
        for other in range(1, spread):
            total = total + part[step, other]

        drive = incident[:, step, :] - total
        high = drive.astype(BF16)
        low = (drive - high.astype(F32)).astype(BF16)
        left = jnp.concatenate(
            [
                jnp.concatenate([high, high], axis=1),
                jnp.concatenate([low, jnp.zeros_like(low)], axis=1),
            ],
            axis=0,
        )

        def solve_part(index, total):
            value = lax.dot_general(left, inverse_cat[index], NT_DIMS, preferred_element_type=F32)
            return total + jnp.where(row == index, value[:boxes] + value[boxes:], 0.0)

        current = jnp.zeros((boxes, width), F32)
        for index in range(boxes):
            current = solve_part(index, current)
        current = current.astype(BF16)
        out[step] = current
        if step < steps - 1:
            cur_all[pl.ds(step * boxes, boxes), :] = current
            win[1, lag_span + step] = current.astype(F32)
            start_window(step + 1)

    for step in range(steps):
        wait_window_sent(step)
        for offset in range(1, peers):
            far_copy(step, offset).wait_send()
        for offset in range(1, spread):
            part_copy(step, offset).wait_send()


def body(
    history_currents,
    history_rays,
    incident,
    near_blocks,
    near_partners,
    self_inverse,
    projection,
    reception,
    translations,
    send_source,
    send_delay,
    send_target,
    send_class,
    slot_counts,
):
    boxes, hist_len, width = history_currents.shape
    rays = history_rays.shape[2]
    steps = incident.shape[1]
    near, lags = near_blocks.shape[1:3]
    peers, dirs, subs = (lax.axis_size(a) for a in ("box", "dir", "sub"))
    spread = dirs * subs
    lag_span = lags * spread
    slots = peers * send_source.shape[2]
    smem = pl.BlockSpec(memory_space=pltpu.SMEM)
    vmem = pl.BlockSpec(memory_space=pltpu.VMEM)
    hbm = pl.BlockSpec(memory_space=pl.ANY)
    dma = pltpu.SemaphoreType.DMA
    currents = pl.pallas_call(
        functools.partial(march, peers, dirs, subs),
        out_shape=jax.ShapeDtypeStruct((steps, boxes, width), BF16),
        in_specs=[smem] * 6 + [vmem] * 2 + [hbm] * 6,
        out_specs=vmem,
        scratch_shapes=[
            pltpu.VMEM((boxes * hist_len, rays), BF16),
            pltpu.VMEM(near_blocks.shape, BF16),
            pltpu.VMEM(self_inverse.shape, F32),
            pltpu.VMEM(projection.shape, BF16),
            pltpu.VMEM(reception.shape, BF16),
            pltpu.VMEM(translations.shape, BF16),
            pltpu.VMEM((boxes, width, 2 * width), BF16),
            pltpu.VMEM((boxes, hist_len, width), F32),
            pltpu.VMEM((3, lag_span + steps, boxes, width), F32),
            pltpu.VMEM((steps * boxes, width), BF16),
            pltpu.VMEM((near * boxes, 3 * boxes), BF16),
            pltpu.VMEM((steps * slots, steps * boxes), BF16),
            pltpu.VMEM((slots, peers * boxes), F32),
            pltpu.VMEM((slots, rays), BF16),
            pltpu.VMEM((steps * slots, width), F32),
            pltpu.VMEM((steps, peers, boxes, width), F32),
            pltpu.VMEM((steps, peers, boxes, width), F32),
            pltpu.VMEM((steps, spread, boxes, width), F32),
            dma((6,)),
            dma((steps, 2)),
            dma((steps, 2)),
            dma((steps, peers)),
            dma((steps, peers)),
            dma((steps, spread)),
            dma((steps, spread)),
        ],
        compiler_params=pltpu.CompilerParams(
            collective_id=0, has_side_effects=True, vmem_limit_bytes=60 * 1024 * 1024
        ),
    )(
        send_source,
        send_delay,
        send_target,
        send_class,
        slot_counts,
        near_partners,
        history_currents,
        incident,
        history_rays.reshape(boxes * hist_len, rays),
        near_blocks,
        self_inverse,
        projection,
        reception,
        translations,
    )
    currents = currents.transpose(1, 0, 2)
    new_rays = jnp.einsum("bts,sk->btk", currents, projection, preferred_element_type=F32)
    return currents, new_rays.astype(BF16)


def solution(mesh):
    return jax.shard_map(
        body,
        mesh=mesh,
        in_specs=(
            P(("groups", "box"), None, None),
            P(("groups", "box"), None, ("dir", "sub")),
            P(("groups", "box"), None, None),
            P("box", None, ("dir", "sub"), None, None),
            P("box", None),
            P("box", None, None),
            P(None, ("dir", "sub")),
            P(("dir", "sub"), None),
            P(None, ("dir", "sub")),
            P("box", None, None),
            P("box", None, None),
            P("box", None, None),
            P("box", None, None),
            P("box", None),
        ),
        out_specs=(P(("groups", "box"), None, None), P(("groups", "box"), None, ("dir", "sub"))),
        check_vma=False,
    )
```

```python
import functools

import jax
import jax.numpy as jnp
from jax import lax
from jax.experimental import pallas as pl
from jax.experimental.pallas import tpu as pltpu
from jax.sharding import PartitionSpec as P

MESH = pl.DeviceIdType.MESH
NT_DIMS = (((1,), (1,)), ((), ()))
F32 = jnp.float32
BF16 = jnp.bfloat16


def march(
    peers,
    dirs,
    subs,
    source_ids,
    delay_ids,
    target_ids,
    class_ids,
    live_counts,
    partner_ids,
    hist_cur,
    incident,
    rays_hbm,
    near_hbm,
    inverse_hbm,
    projection_hbm,
    reception_hbm,
    translations_hbm,
    out,
    hist_rays,
    near_v,
    near_t,
    inverse_v,
    projection,
    reception,
    translations,
    inverse_cat,
    hist_f32,
    win,
    cur_all,
    near_pick,
    new_pick,
    target_pick,
    factors,
    hist_terms,
    far_send,
    far_recv,
    part,
    copy_sems,
    win_send_sem,
    win_recv_sem,
    far_send_sem,
    far_recv_sem,
    part_send_sem,
    part_recv_sem,
):
    boxes, steps, width = incident.shape
    hist_len = hist_cur.shape[1]
    lags = near_v.shape[2]
    near = near_v.shape[1]
    rays = projection.shape[1]
    capacity = source_ids.shape[2]
    slots = peers * capacity
    spread = dirs * subs
    lag_span = lags * spread
    box = lax.axis_index("box")
    piece = lax.axis_index("dir") * subs + lax.axis_index("sub")
    chunk = 512 if rays % 512 == 0 else (256 if rays % 256 == 0 else 128)

    copies = [
        pltpu.make_async_copy(src, dst, copy_sems.at[i])
        for i, (src, dst) in enumerate(
            (
                (translations_hbm, translations),
                (rays_hbm, hist_rays),
                (reception_hbm, reception),
                (inverse_hbm, inverse_v),
                (near_hbm, near_v),
                (projection_hbm, projection),
            )
        )
    ]
    for copy in copies[:3]:
        copy.start()

    def peer_of(offset):
        return {"box": lax.rem(box + offset, peers)}

    def sibling_of(offset):
        other = lax.rem(piece + offset, spread)
        return {"dir": other // subs, "sub": lax.rem(other, subs)}

    hist_f32[...] = hist_cur[...].astype(F32)
    for back in range(lag_span):
        win[1, back] = hist_f32[:, hist_len - lag_span + back, :]
    win[0] = jnp.zeros(win.shape[1:], F32)
    win[2] = jnp.zeros(win.shape[1:], F32)
    cur_all[...] = jnp.zeros(cur_all.shape, BF16)

    barrier = pltpu.get_barrier_semaphore()
    for offset in range(1, peers):
        pl.semaphore_signal(barrier, inc=1, device_id=peer_of(offset), device_id_type=MESH)
    for offset in range(1, spread):
        pl.semaphore_signal(barrier, inc=1, device_id=sibling_of(offset), device_id_type=MESH)


    def column_of(count, value):
        tiles = []
        rows = lax.broadcasted_iota(jnp.int32, (8, 1), 0)
        for start in range(0, count, 8):
            tile = jnp.full((8, 1), -1, jnp.int32)
            for i in range(min(8, count - start)):
                tile = jnp.where(rows == i, value(start + i), tile)
            tiles.append(tile)
        return jnp.concatenate(tiles, axis=0)[:count]

    def pick(ids, size):
        lanes = lax.broadcasted_iota(jnp.int32, (ids.shape[0], size), 1)
        return jnp.where(lanes == ids, 1.0, 0.0)

    def slot_of(ref):
        return column_of(slots, lambda j: ref[0, j // capacity, j % capacity])

    source, delay = slot_of(source_ids), slot_of(delay_ids)
    hist_rows = []
    new_rows = []
    for step in range(steps):
        back = step - delay
        hist_rows.append(jnp.where(back < 0, source * hist_len + hist_len + back, -1))
        new_rows.append(jnp.where(back >= 0, back * boxes + source, -1))
    hist_pick = pick(jnp.concatenate(hist_rows, axis=0), boxes * hist_len).astype(BF16)
    new_pick[...] = pick(jnp.concatenate(new_rows, axis=0), steps * boxes).astype(BF16)
    class_pick = pick(slot_of(class_ids), translations.shape[0]).astype(BF16)
    live = column_of(slots, lambda j: live_counts[0, j // capacity])
    place = lax.broadcasted_iota(jnp.int32, (slots, 1), 0)
    dest = jnp.where(place % capacity < live, place // capacity * boxes + slot_of(target_ids), -1)
    chosen = pick(dest, peers * boxes)
    target_pick[...] = jnp.concatenate([chosen, chosen], axis=0).T.astype(BF16)
    partner = column_of(near * boxes, lambda j: partner_ids[j % boxes, j // boxes])
    near_pick[...] = pick(partner - (box - 1) * boxes, 3 * boxes).astype(BF16)
    for copy in copies[3:]:
        copy.start()
    pl.semaphore_wait(barrier, peers - 1 + spread - 1)

    def window_copy(order, side):
        span = pl.ds(0, lag_span) if order == 0 else pl.ds(lag_span + order - 1, 1)
        offset = 1 if side == 0 else peers - 1
        return pltpu.make_async_remote_copy(
            src_ref=win.at[1, span],
            dst_ref=win.at[0 if side == 0 else 2, span],
            send_sem=win_send_sem.at[order, side],
            recv_sem=win_recv_sem.at[order, side],
            device_id=peer_of(offset),
            device_id_type=MESH,
        )

    has_next = box < peers - 1
    has_prev = box > 0

    def start_window(order):
        @pl.when(has_next)
        def _():
            window_copy(order, 0).start()

        @pl.when(has_prev)
        def _():
            window_copy(order, 1).start()

    def wait_window(order):
        @pl.when(has_prev)
        def _():
            window_copy(order, 0).wait_recv()

        @pl.when(has_next)
        def _():
            window_copy(order, 1).wait_recv()

    def wait_window_sent(order):
        @pl.when(has_next)
        def _():
            window_copy(order, 0).wait_send()

        @pl.when(has_prev)
        def _():
            window_copy(order, 1).wait_send()

    start_window(0)

    def far_copy(step, offset):
        return pltpu.make_async_remote_copy(
            src_ref=far_send.at[step, lax.rem(box + offset, peers)],
            dst_ref=far_recv.at[step, offset],
            send_sem=far_send_sem.at[step, offset],
            recv_sem=far_recv_sem.at[step, offset],
            device_id=peer_of(offset),
            device_id_type=MESH,
        )

    def part_copy(step, offset):
        return pltpu.make_async_remote_copy(
            src_ref=part.at[step, piece],
            dst_ref=part.at[step, piece],
            send_sem=part_send_sem.at[step, offset],
            recv_sem=part_recv_sem.at[step, offset],
            device_id=sibling_of(offset),
            device_id_type=MESH,
        )

    def columns(index):
        return pl.ds(index * chunk, chunk)

    def history_part(index, total):
        at = columns(index)
        factor = jnp.dot(class_pick, translations[:, at], preferred_element_type=F32).astype(BF16)
        factors[:, at] = factor
        picked = jnp.dot(hist_pick, hist_rays[:, at], preferred_element_type=F32).astype(BF16)
        terms = jnp.concatenate(
            [picked[t * slots : (t + 1) * slots] * factor for t in range(steps)], axis=0
        )
        return total + jnp.dot(terms, reception[at, :], preferred_element_type=F32)

    for copy in copies[:3]:
        copy.wait()
    total = jnp.zeros((steps * slots, width), F32)
    for index in range(rays // chunk):
        total = history_part(index, total)
    hist_terms[...] = total

    def send_far(step):
        terms = hist_terms[pl.ds(step * slots, slots), :]
        if step > 0:
            picked = jnp.dot(
                new_pick[pl.ds(step * slots, slots), :], cur_all[...], preferred_element_type=F32
            ).astype(BF16)

            def new_part(index, total):
                at = columns(index)
                ray = jnp.dot(picked, projection[:, at], preferred_element_type=F32).astype(BF16)
                return total + jnp.dot(
                    ray * factors[:, at], reception[at, :], preferred_element_type=F32
                )

            for index in range(rays // chunk):
                terms = new_part(index, terms)
        high = terms.astype(BF16)
        low = (terms - high.astype(F32)).astype(BF16)
        far = jnp.dot(
            target_pick[...], jnp.concatenate([high, low], axis=0), preferred_element_type=F32
        )
        far_send[step] = far.reshape(peers, boxes, width)
        for offset in range(1, peers):
            far_copy(step, offset).start()

    row = lax.broadcasted_iota(jnp.int32, (boxes, width), 0)

    for step in range(steps):
        send_far(step)
        if step == 0:
            copies[3].wait()

            def split(index, carry):
                whole = inverse_v[index].T
                high = whole.astype(BF16)
                low = (whole - high.astype(F32)).astype(BF16)
                inverse_cat[index] = jnp.concatenate([high, low], axis=0)
                return carry

            lax.fori_loop(0, boxes, split, 0)
            copies[4].wait()
            copies[5].wait()
        wait_window(step)

        pieces = []
        for lag in range(lags):
            at = lag_span + step - (piece * lags + lag + 1)
            table = jnp.concatenate([win[0, at], win[1, at], win[2, at]], axis=0).astype(BF16)
            gathered = jnp.dot(near_pick[...], table, preferred_element_type=F32).astype(BF16)
            for n in range(near):
                pieces.append(gathered[n * boxes : (n + 1) * boxes])
        sources = jnp.concatenate(pieces, axis=1)

        def near_part(index, total):
            if step > 0:
                value = jnp.dot(sources, near_t[index], preferred_element_type=F32)
                return total + jnp.where(row == index, value, 0.0)
            blocks = jnp.concatenate(
                [near_v[index, n, lag] for lag in range(lags) for n in range(near)], axis=1
            )
            value = lax.dot_general(sources, blocks, NT_DIMS, preferred_element_type=F32)
            return total + jnp.where(row == index, value, 0.0)

        field = jnp.zeros((boxes, width), F32)
        for index in range(boxes):
            field = near_part(index, field)
        field = field + far_send[step, box]
        for offset in range(1, peers):
            far_copy(step, offset).wait_recv()
            field = field + far_recv[step, offset]
        part[step, piece] = field
        for offset in range(1, spread):
            part_copy(step, offset).start()
        if step == 0:

            def turn(index, carry):
                for lag in range(lags):
                    for n in range(near):
                        start = (lag * near + n) * width
                        near_t[index, pl.ds(start, width), :] = near_v[index, n, lag].T
                return carry

            lax.fori_loop(0, boxes, turn, 0)
        for offset in range(1, spread):
            part_copy(step, offset).wait_recv()
        total = part[step, 0]
        for other in range(1, spread):
            total = total + part[step, other]

        drive = incident[:, step, :] - total
        high = drive.astype(BF16)
        low = (drive - high.astype(F32)).astype(BF16)
        left = jnp.concatenate(
            [
                jnp.concatenate([high, high], axis=1),
                jnp.concatenate([low, jnp.zeros_like(low)], axis=1),
            ],
            axis=0,
        )

        def solve_part(index, total):
            value = jnp.dot(left, inverse_cat[index], preferred_element_type=F32)
            return total + jnp.where(row == index, value[:boxes] + value[boxes:], 0.0)

        current = jnp.zeros((boxes, width), F32)
        for index in range(boxes):
            current = solve_part(index, current)
        current = current.astype(BF16)
        out[step] = current
        if step < steps - 1:
            cur_all[pl.ds(step * boxes, boxes), :] = current
            win[1, lag_span + step] = current.astype(F32)
            start_window(step + 1)

    for step in range(steps):
        wait_window_sent(step)
        for offset in range(1, peers):
            far_copy(step, offset).wait_send()
        for offset in range(1, spread):
            part_copy(step, offset).wait_send()


def body(
    history_currents,
    history_rays,
    incident,
    near_blocks,
    near_partners,
    self_inverse,
    projection,
    reception,
    translations,
    send_source,
    send_delay,
    send_target,
    send_class,
    slot_counts,
):
    boxes, hist_len, width = history_currents.shape
    rays = history_rays.shape[2]
    steps = incident.shape[1]
    near, lags = near_blocks.shape[1:3]
    peers, dirs, subs = (lax.axis_size(a) for a in ("box", "dir", "sub"))
    spread = dirs * subs
    lag_span = lags * spread
    slots = peers * send_source.shape[2]
    smem = pl.BlockSpec(memory_space=pltpu.SMEM)
    vmem = pl.BlockSpec(memory_space=pltpu.VMEM)
    hbm = pl.BlockSpec(memory_space=pl.ANY)
    dma = pltpu.SemaphoreType.DMA
    currents = pl.pallas_call(
        functools.partial(march, peers, dirs, subs),
        out_shape=jax.ShapeDtypeStruct((steps, boxes, width), BF16),
        in_specs=[smem] * 6 + [vmem] * 2 + [hbm] * 6,
        out_specs=vmem,
        scratch_shapes=[
            pltpu.VMEM((boxes * hist_len, rays), BF16),
            pltpu.VMEM(near_blocks.shape, BF16),
            pltpu.VMEM((boxes, lags * near * width, width), BF16),
            pltpu.VMEM(self_inverse.shape, F32),
            pltpu.VMEM(projection.shape, BF16),
            pltpu.VMEM(reception.shape, BF16),
            pltpu.VMEM(translations.shape, BF16),
            pltpu.VMEM((boxes, 2 * width, width), BF16),
            pltpu.VMEM((boxes, hist_len, width), F32),
            pltpu.VMEM((3, lag_span + steps, boxes, width), F32),
            pltpu.VMEM((steps * boxes, width), BF16),
            pltpu.VMEM((near * boxes, 3 * boxes), BF16),
            pltpu.VMEM((steps * slots, steps * boxes), BF16),
            pltpu.VMEM((peers * boxes, 2 * slots), BF16),
            pltpu.VMEM((slots, rays), BF16),
            pltpu.VMEM((steps * slots, width), F32),
            pltpu.VMEM((steps, peers, boxes, width), F32),
            pltpu.VMEM((steps, peers, boxes, width), F32),
            pltpu.VMEM((steps, spread, boxes, width), F32),
            dma((6,)),
            dma((steps, 2)),
            dma((steps, 2)),
            dma((steps, peers)),
            dma((steps, peers)),
            dma((steps, spread)),
            dma((steps, spread)),
        ],
        compiler_params=pltpu.CompilerParams(
            collective_id=0, has_side_effects=True, vmem_limit_bytes=60 * 1024 * 1024
        ),
    )(
        send_source,
        send_delay,
        send_target,
        send_class,
        slot_counts,
        near_partners,
        history_currents,
        incident,
        history_rays.reshape(boxes * hist_len, rays),
        near_blocks,
        self_inverse,
        projection,
        reception,
        translations,
    )
    currents = currents.transpose(1, 0, 2)
    new_rays = jnp.einsum("bts,sk->btk", currents, projection, preferred_element_type=F32)
    return currents, new_rays.astype(BF16)


def solution(mesh):
    return jax.shard_map(
        body,
        mesh=mesh,
        in_specs=(
            P(("groups", "box"), None, None),
            P(("groups", "box"), None, ("dir", "sub")),
            P(("groups", "box"), None, None),
            P("box", None, ("dir", "sub"), None, None),
            P("box", None),
            P("box", None, None),
            P(None, ("dir", "sub")),
            P(("dir", "sub"), None),
            P(None, ("dir", "sub")),
            P("box", None, None),
            P("box", None, None),
            P("box", None, None),
            P("box", None, None),
            P("box", None),
        ),
        out_specs=(P(("groups", "box"), None, None), P(("groups", "box"), None, ("dir", "sub"))),
        check_vma=False,
    )
```

```python
import functools

import jax
import jax.numpy as jnp
from jax import lax
from jax.experimental import pallas as pl
from jax.experimental.pallas import tpu as pltpu
from jax.sharding import PartitionSpec as P

MESH = pl.DeviceIdType.MESH
NT_DIMS = (((1,), (1,)), ((), ()))
F32 = jnp.float32
BF16 = jnp.bfloat16


def march(
    peers,
    dirs,
    subs,
    source_ids,
    delay_ids,
    target_ids,
    class_ids,
    live_counts,
    partner_ids,
    hist_cur,
    incident,
    rays_hbm,
    near_hbm,
    inverse_hbm,
    projection_hbm,
    reception_hbm,
    translations_hbm,
    out,
    hist_rays,
    near_v,
    near_t,
    inverse_v,
    projection,
    reception,
    translations,
    inverse_cat,
    hist_f32,
    win,
    cur_all,
    near_pick,
    new_pick,
    target_pick,
    factors,
    hist_terms,
    far_send,
    far_recv,
    part,
    copy_sems,
    win_send_sem,
    win_recv_sem,
    far_send_sem,
    far_recv_sem,
    part_send_sem,
    part_recv_sem,
):
    boxes, steps, width = incident.shape
    hist_len = hist_cur.shape[1]
    lags = near_v.shape[2]
    near = near_v.shape[1]
    rays = projection.shape[1]
    capacity = source_ids.shape[2]
    slots = peers * capacity
    spread = dirs * subs
    lag_span = lags * spread
    box = lax.axis_index("box")
    piece = lax.axis_index("dir") * subs + lax.axis_index("sub")
    chunk = 512 if rays % 512 == 0 else (256 if rays % 256 == 0 else 128)

    copies = [
        pltpu.make_async_copy(src, dst, copy_sems.at[i])
        for i, (src, dst) in enumerate(
            (
                (translations_hbm, translations),
                (rays_hbm, hist_rays),
                (reception_hbm, reception),
                (inverse_hbm, inverse_v),
                (near_hbm, near_v),
                (projection_hbm, projection),
            )
        )
    ]
    for copy in copies[:3]:
        copy.start()

    def peer_of(offset):
        return {"box": lax.rem(box + offset, peers)}

    def sibling_of(offset):
        other = lax.rem(piece + offset, spread)
        return {"dir": other // subs, "sub": lax.rem(other, subs)}

    hist_f32[...] = hist_cur[...].astype(F32)
    for back in range(lag_span):
        win[1, back] = hist_f32[:, hist_len - lag_span + back, :]
    win[0] = jnp.zeros(win.shape[1:], F32)
    win[2] = jnp.zeros(win.shape[1:], F32)
    cur_all[...] = jnp.zeros(cur_all.shape, BF16)

    barrier = pltpu.get_barrier_semaphore()
    for offset in range(1, peers):
        for turn_by in range(spread):
            target = {**peer_of(offset), **sibling_of(turn_by)}
            pl.semaphore_signal(barrier, inc=1, device_id=target, device_id_type=MESH)
    for offset in range(1, spread):
        pl.semaphore_signal(barrier, inc=1, device_id=sibling_of(offset), device_id_type=MESH)


    def column_of(count, value):
        tiles = []
        rows = lax.broadcasted_iota(jnp.int32, (8, 1), 0)
        for start in range(0, count, 8):
            tile = jnp.full((8, 1), -1, jnp.int32)
            for i in range(min(8, count - start)):
                tile = jnp.where(rows == i, value(start + i), tile)
            tiles.append(tile)
        return jnp.concatenate(tiles, axis=0)[:count]

    def pick(ids, size):
        lanes = lax.broadcasted_iota(jnp.int32, (ids.shape[0], size), 1)
        return jnp.where(lanes == ids, 1.0, 0.0)

    def slot_of(ref):
        return column_of(slots, lambda j: ref[0, j // capacity, j % capacity])

    source, delay = slot_of(source_ids), slot_of(delay_ids)
    hist_rows = []
    new_rows = []
    for step in range(steps):
        back = step - delay
        hist_rows.append(jnp.where(back < 0, source * hist_len + hist_len + back, -1))
        new_rows.append(jnp.where(back >= 0, back * boxes + source, -1))
    hist_pick = pick(jnp.concatenate(hist_rows, axis=0), boxes * hist_len).astype(BF16)
    new_pick[...] = pick(jnp.concatenate(new_rows, axis=0), steps * boxes).astype(BF16)
    class_pick = pick(slot_of(class_ids), translations.shape[0]).astype(BF16)
    live = column_of(slots, lambda j: live_counts[0, j // capacity])
    place = lax.broadcasted_iota(jnp.int32, (slots, 1), 0)
    dest = jnp.where(place % capacity < live, place // capacity * boxes + slot_of(target_ids), -1)
    chosen = pick(dest, peers * boxes)
    target_pick[...] = jnp.concatenate([chosen, chosen], axis=0).T.astype(BF16)
    partner = column_of(near * boxes, lambda j: partner_ids[j % boxes, j // boxes])
    near_pick[...] = pick(partner - (box - 1) * boxes, 3 * boxes).astype(BF16)
    for copy in copies[3:]:
        copy.start()
    pl.semaphore_wait(barrier, peers * spread - 1)

    def window_copy(order, side):
        span = pl.ds(0, lag_span) if order == 0 else pl.ds(lag_span + order - 1, 1)
        offset = 1 if side == 0 else peers - 1
        return pltpu.make_async_remote_copy(
            src_ref=win.at[1, span],
            dst_ref=win.at[0 if side == 0 else 2, span],
            send_sem=win_send_sem.at[order, side],
            recv_sem=win_recv_sem.at[order, side],
            device_id=peer_of(offset),
            device_id_type=MESH,
        )

    has_next = box < peers - 1
    has_prev = box > 0

    def start_window(order):
        @pl.when(has_next)
        def _():
            window_copy(order, 0).start()

        @pl.when(has_prev)
        def _():
            window_copy(order, 1).start()

    def wait_window(order):
        @pl.when(has_prev)
        def _():
            window_copy(order, 0).wait_recv()

        @pl.when(has_next)
        def _():
            window_copy(order, 1).wait_recv()

    def wait_window_sent(order):
        @pl.when(has_next)
        def _():
            window_copy(order, 0).wait_send()

        @pl.when(has_prev)
        def _():
            window_copy(order, 1).wait_send()

    start_window(0)

    def far_copy(step, offset, turn_by):
        return pltpu.make_async_remote_copy(
            src_ref=far_send.at[step, lax.rem(box + offset, peers)],
            dst_ref=far_recv.at[step, offset, piece],
            send_sem=far_send_sem.at[step, offset * spread + turn_by],
            recv_sem=far_recv_sem.at[step, offset * spread + turn_by],
            device_id={**peer_of(offset), **sibling_of(turn_by)},
            device_id_type=MESH,
        )

    def part_copy(step, offset):
        return pltpu.make_async_remote_copy(
            src_ref=part.at[step, piece],
            dst_ref=part.at[step, piece],
            send_sem=part_send_sem.at[step, offset],
            recv_sem=part_recv_sem.at[step, offset],
            device_id=sibling_of(offset),
            device_id_type=MESH,
        )

    def columns(index):
        return pl.ds(index * chunk, chunk)

    def history_part(index, total):
        at = columns(index)
        factor = jnp.dot(class_pick, translations[:, at], preferred_element_type=F32).astype(BF16)
        factors[:, at] = factor
        picked = jnp.dot(hist_pick, hist_rays[:, at], preferred_element_type=F32).astype(BF16)
        terms = jnp.concatenate(
            [picked[t * slots : (t + 1) * slots] * factor for t in range(steps)], axis=0
        )
        return total + jnp.dot(terms, reception[at, :], preferred_element_type=F32)

    for copy in copies[:3]:
        copy.wait()
    total = jnp.zeros((steps * slots, width), F32)
    for index in range(rays // chunk):
        total = history_part(index, total)
    hist_terms[...] = total

    def send_far(step):
        terms = hist_terms[pl.ds(step * slots, slots), :]
        if step > 0:
            picked = jnp.dot(
                new_pick[pl.ds(step * slots, slots), :], cur_all[...], preferred_element_type=F32
            ).astype(BF16)

            def new_part(index, total):
                at = columns(index)
                ray = jnp.dot(picked, projection[:, at], preferred_element_type=F32).astype(BF16)
                return total + jnp.dot(
                    ray * factors[:, at], reception[at, :], preferred_element_type=F32
                )

            for index in range(rays // chunk):
                terms = new_part(index, terms)
        high = terms.astype(BF16)
        low = (terms - high.astype(F32)).astype(BF16)
        far = jnp.dot(
            target_pick[...], jnp.concatenate([high, low], axis=0), preferred_element_type=F32
        )
        far_send[step] = far.astype(BF16).reshape(peers, boxes, width)
        for offset in range(1, peers):
            for turn_by in range(spread):
                far_copy(step, offset, turn_by).start()

    row = lax.broadcasted_iota(jnp.int32, (boxes, width), 0)

    for step in range(steps):
        send_far(step)
        if step == 0:
            copies[3].wait()

            def split(index, carry):
                whole = inverse_v[index].T
                high = whole.astype(BF16)
                low = (whole - high.astype(F32)).astype(BF16)
                inverse_cat[index] = jnp.concatenate([high, low], axis=0)
                return carry

            lax.fori_loop(0, boxes, split, 0)
            copies[4].wait()
            copies[5].wait()
        wait_window(step)

        pieces = []
        for lag in range(lags):
            at = lag_span + step - (piece * lags + lag + 1)
            table = jnp.concatenate([win[0, at], win[1, at], win[2, at]], axis=0).astype(BF16)
            gathered = jnp.dot(near_pick[...], table, preferred_element_type=F32).astype(BF16)
            for n in range(near):
                pieces.append(gathered[n * boxes : (n + 1) * boxes])
        sources = jnp.concatenate(pieces, axis=1)

        def near_part(index, total):
            if step > 0:
                value = jnp.dot(sources, near_t[index], preferred_element_type=F32)
                return total + jnp.where(row == index, value, 0.0)
            blocks = jnp.concatenate(
                [near_v[index, n, lag] for lag in range(lags) for n in range(near)], axis=1
            )
            value = lax.dot_general(sources, blocks, NT_DIMS, preferred_element_type=F32)
            return total + jnp.where(row == index, value, 0.0)

        field = jnp.zeros((boxes, width), F32)
        for index in range(boxes):
            field = near_part(index, field)
        part[step, piece] = field + far_send[step, box].astype(F32)
        for offset in range(1, spread):
            part_copy(step, offset).start()
        if step == 0:

            def turn(index, carry):
                for lag in range(lags):
                    for n in range(near):
                        start = (lag * near + n) * width
                        near_t[index, pl.ds(start, width), :] = near_v[index, n, lag].T
                return carry

            lax.fori_loop(0, boxes, turn, 0)
        for offset in range(1, peers):
            for turn_by in range(spread):
                far_copy(step, offset, turn_by).wait_recv()
        around = jnp.zeros((boxes, width), F32)
        for offset in range(1, peers):
            for other in range(spread):
                around = around + far_recv[step, offset, other].astype(F32)
        for offset in range(1, spread):
            part_copy(step, offset).wait_recv()
        total = around + part[step, 0]
        for other in range(1, spread):
            total = total + part[step, other]

        drive = incident[:, step, :] - total
        high = drive.astype(BF16)
        low = (drive - high.astype(F32)).astype(BF16)
        left = jnp.concatenate(
            [
                jnp.concatenate([high, high], axis=1),
                jnp.concatenate([low, jnp.zeros_like(low)], axis=1),
            ],
            axis=0,
        )

        def solve_part(index, total):
            value = jnp.dot(left, inverse_cat[index], preferred_element_type=F32)
            return total + jnp.where(row == index, value[:boxes] + value[boxes:], 0.0)

        current = jnp.zeros((boxes, width), F32)
        for index in range(boxes):
            current = solve_part(index, current)
        current = current.astype(BF16)
        out[step] = current
        if step < steps - 1:
            cur_all[pl.ds(step * boxes, boxes), :] = current
            win[1, lag_span + step] = current.astype(F32)
            start_window(step + 1)

    for step in range(steps):
        wait_window_sent(step)
        for offset in range(1, peers):
            for turn_by in range(spread):
                far_copy(step, offset, turn_by).wait_send()
        for offset in range(1, spread):
            part_copy(step, offset).wait_send()


def body(
    history_currents,
    history_rays,
    incident,
    near_blocks,
    near_partners,
    self_inverse,
    projection,
    reception,
    translations,
    send_source,
    send_delay,
    send_target,
    send_class,
    slot_counts,
):
    boxes, hist_len, width = history_currents.shape
    rays = history_rays.shape[2]
    steps = incident.shape[1]
    near, lags = near_blocks.shape[1:3]
    peers, dirs, subs = (lax.axis_size(a) for a in ("box", "dir", "sub"))
    spread = dirs * subs
    lag_span = lags * spread
    slots = peers * send_source.shape[2]
    smem = pl.BlockSpec(memory_space=pltpu.SMEM)
    vmem = pl.BlockSpec(memory_space=pltpu.VMEM)
    hbm = pl.BlockSpec(memory_space=pl.ANY)
    dma = pltpu.SemaphoreType.DMA
    currents = pl.pallas_call(
        functools.partial(march, peers, dirs, subs),
        out_shape=jax.ShapeDtypeStruct((steps, boxes, width), BF16),
        in_specs=[smem] * 6 + [vmem] * 2 + [hbm] * 6,
        out_specs=vmem,
        scratch_shapes=[
            pltpu.VMEM((boxes * hist_len, rays), BF16),
            pltpu.VMEM(near_blocks.shape, BF16),
            pltpu.VMEM((boxes, lags * near * width, width), BF16),
            pltpu.VMEM(self_inverse.shape, F32),
            pltpu.VMEM(projection.shape, BF16),
            pltpu.VMEM(reception.shape, BF16),
            pltpu.VMEM(translations.shape, BF16),
            pltpu.VMEM((boxes, 2 * width, width), BF16),
            pltpu.VMEM((boxes, hist_len, width), F32),
            pltpu.VMEM((3, lag_span + steps, boxes, width), F32),
            pltpu.VMEM((steps * boxes, width), BF16),
            pltpu.VMEM((near * boxes, 3 * boxes), BF16),
            pltpu.VMEM((steps * slots, steps * boxes), BF16),
            pltpu.VMEM((peers * boxes, 2 * slots), BF16),
            pltpu.VMEM((slots, rays), BF16),
            pltpu.VMEM((steps * slots, width), F32),
            pltpu.VMEM((steps, peers, boxes, width), BF16),
            pltpu.VMEM((steps, peers, spread, boxes, width), BF16),
            pltpu.VMEM((steps, spread, boxes, width), F32),
            dma((6,)),
            dma((steps, 2)),
            dma((steps, 2)),
            dma((steps, peers * spread)),
            dma((steps, peers * spread)),
            dma((steps, spread)),
            dma((steps, spread)),
        ],
        compiler_params=pltpu.CompilerParams(
            collective_id=0, has_side_effects=True, vmem_limit_bytes=60 * 1024 * 1024
        ),
    )(
        send_source,
        send_delay,
        send_target,
        send_class,
        slot_counts,
        near_partners,
        history_currents,
        incident,
        history_rays.reshape(boxes * hist_len, rays),
        near_blocks,
        self_inverse,
        projection,
        reception,
        translations,
    )
    currents = currents.transpose(1, 0, 2)
    new_rays = jnp.einsum("bts,sk->btk", currents, projection, preferred_element_type=F32)
    return currents, new_rays.astype(BF16)


def solution(mesh):
    return jax.shard_map(
        body,
        mesh=mesh,
        in_specs=(
            P(("groups", "box"), None, None),
            P(("groups", "box"), None, ("dir", "sub")),
            P(("groups", "box"), None, None),
            P("box", None, ("dir", "sub"), None, None),
            P("box", None),
            P("box", None, None),
            P(None, ("dir", "sub")),
            P(("dir", "sub"), None),
            P(None, ("dir", "sub")),
            P("box", None, None),
            P("box", None, None),
            P("box", None, None),
            P("box", None, None),
            P("box", None),
        ),
        out_specs=(P(("groups", "box"), None, None), P(("groups", "box"), None, ("dir", "sub"))),
        check_vma=False,
    )
```

```python
import functools

import jax
import jax.numpy as jnp
from jax import lax
from jax.experimental import pallas as pl
from jax.experimental.pallas import tpu as pltpu
from jax.sharding import PartitionSpec as P

MESH = pl.DeviceIdType.MESH
NT_DIMS = (((1,), (1,)), ((), ()))
F32 = jnp.float32
BF16 = jnp.bfloat16


def march(
    peers,
    dirs,
    subs,
    source_ids,
    delay_ids,
    target_ids,
    class_ids,
    live_counts,
    partner_ids,
    hist_cur,
    incident,
    rays_hbm,
    near_hbm,
    inverse_hbm,
    projection_hbm,
    reception_hbm,
    translations_hbm,
    out,
    hist_rays,
    near_v,
    near_t,
    inverse_v,
    projection,
    reception,
    translations,
    inverse_cat,
    hist_f32,
    win,
    cur_all,
    near_pick,
    new_pick,
    target_pick,
    factors,
    hist_terms,
    far_send,
    far_recv,
    part,
    copy_sems,
    win_send_sem,
    win_recv_sem,
    far_send_sem,
    far_recv_sem,
    part_send_sem,
    part_recv_sem,
):
    boxes, steps, width = incident.shape
    hist_len = hist_cur.shape[1]
    lags = near_v.shape[2]
    near = near_v.shape[1]
    rays = projection.shape[1]
    capacity = source_ids.shape[2]
    slots = peers * capacity
    spread = dirs * subs
    lag_span = lags * spread
    box = lax.axis_index("box")
    piece = lax.axis_index("dir") * subs + lax.axis_index("sub")
    chunk = 512 if rays % 512 == 0 else (256 if rays % 256 == 0 else 128)

    copies = [
        pltpu.make_async_copy(src, dst, copy_sems.at[i])
        for i, (src, dst) in enumerate(
            (
                (translations_hbm, translations),
                (rays_hbm, hist_rays),
                (reception_hbm, reception),
                (inverse_hbm, inverse_v),
                (near_hbm, near_v),
                (projection_hbm, projection),
            )
        )
    ]
    for copy in copies[:3]:
        copy.start()

    def peer_of(offset):
        return {"box": lax.rem(box + offset, peers)}

    def sibling_of(offset):
        other = lax.rem(piece + offset, spread)
        return {"dir": other // subs, "sub": lax.rem(other, subs)}

    hist_f32[...] = hist_cur[...].astype(F32)
    for back in range(lag_span):
        win[1, back] = hist_f32[:, hist_len - lag_span + back, :]
    win[0] = jnp.zeros(win.shape[1:], F32)
    win[2] = jnp.zeros(win.shape[1:], F32)
    cur_all[...] = jnp.zeros(cur_all.shape, BF16)

    barrier = pltpu.get_barrier_semaphore()
    for offset in range(1, peers):
        for turn_by in range(spread):
            target = {**peer_of(offset), **sibling_of(turn_by)}
            pl.semaphore_signal(barrier, inc=1, device_id=target, device_id_type=MESH)
    for offset in range(1, spread):
        pl.semaphore_signal(barrier, inc=1, device_id=sibling_of(offset), device_id_type=MESH)


    def column_of(count, value):
        tiles = []
        rows = lax.broadcasted_iota(jnp.int32, (8, 1), 0)
        for start in range(0, count, 8):
            tile = jnp.full((8, 1), -1, jnp.int32)
            for i in range(min(8, count - start)):
                tile = jnp.where(rows == i, value(start + i), tile)
            tiles.append(tile)
        return jnp.concatenate(tiles, axis=0)[:count]

    def pick(ids, size):
        lanes = lax.broadcasted_iota(jnp.int32, (ids.shape[0], size), 1)
        return jnp.where(lanes == ids, 1.0, 0.0)

    def slot_of(ref):
        return column_of(slots, lambda j: ref[0, j // capacity, j % capacity])

    source, delay = slot_of(source_ids), slot_of(delay_ids)
    hist_rows = []
    new_rows = []
    for step in range(steps):
        back = step - delay
        hist_rows.append(jnp.where(back < 0, source * hist_len + hist_len + back, -1))
        new_rows.append(jnp.where(back >= 0, back * boxes + source, -1))
    hist_pick = pick(jnp.concatenate(hist_rows, axis=0), boxes * hist_len).astype(BF16)
    new_pick[...] = pick(jnp.concatenate(new_rows, axis=0), steps * boxes).astype(BF16)
    class_pick = pick(slot_of(class_ids), translations.shape[0]).astype(BF16)
    live = column_of(slots, lambda j: live_counts[0, j // capacity])
    place = lax.broadcasted_iota(jnp.int32, (slots, 1), 0)
    dest = jnp.where(place % capacity < live, place // capacity * boxes + slot_of(target_ids), -1)
    chosen = pick(dest, peers * boxes)
    target_pick[...] = jnp.concatenate([chosen, chosen], axis=0).T.astype(BF16)
    partner = column_of(near * boxes, lambda j: partner_ids[j % boxes, j // boxes])
    near_pick[...] = pick(partner - (box - 1) * boxes, 3 * boxes).astype(BF16)
    for copy in copies[3:]:
        copy.start()
    pl.semaphore_wait(barrier, peers * spread - 1)

    def window_copy(order, side):
        span = pl.ds(0, lag_span) if order == 0 else pl.ds(lag_span + order - 1, 1)
        offset = 1 if side == 0 else peers - 1
        return pltpu.make_async_remote_copy(
            src_ref=win.at[1, span],
            dst_ref=win.at[0 if side == 0 else 2, span],
            send_sem=win_send_sem.at[order, side],
            recv_sem=win_recv_sem.at[order, side],
            device_id=peer_of(offset),
            device_id_type=MESH,
        )

    has_next = box < peers - 1
    has_prev = box > 0

    def start_window(order):
        @pl.when(has_next)
        def _():
            window_copy(order, 0).start()

        @pl.when(has_prev)
        def _():
            window_copy(order, 1).start()

    def wait_window(order):
        @pl.when(has_prev)
        def _():
            window_copy(order, 0).wait_recv()

        @pl.when(has_next)
        def _():
            window_copy(order, 1).wait_recv()

    def wait_window_sent(order):
        @pl.when(has_next)
        def _():
            window_copy(order, 0).wait_send()

        @pl.when(has_prev)
        def _():
            window_copy(order, 1).wait_send()

    start_window(0)

    def far_copy(step, offset, turn_by):
        return pltpu.make_async_remote_copy(
            src_ref=far_send.at[step, lax.rem(box + offset, peers)],
            dst_ref=far_recv.at[step, offset, piece],
            send_sem=far_send_sem.at[step, offset * spread + turn_by],
            recv_sem=far_recv_sem.at[step, offset * spread + turn_by],
            device_id={**peer_of(offset), **sibling_of(turn_by)},
            device_id_type=MESH,
        )

    def part_copy(step, offset):
        return pltpu.make_async_remote_copy(
            src_ref=part.at[step, piece],
            dst_ref=part.at[step, piece],
            send_sem=part_send_sem.at[step, offset],
            recv_sem=part_recv_sem.at[step, offset],
            device_id=sibling_of(offset),
            device_id_type=MESH,
        )

    def columns(index):
        return pl.ds(index * chunk, chunk)

    def history_part(index, total):
        at = columns(index)
        factor = jnp.dot(class_pick, translations[:, at], preferred_element_type=F32).astype(BF16)
        factors[:, at] = factor
        picked = jnp.dot(hist_pick, hist_rays[:, at], preferred_element_type=F32).astype(BF16)
        terms = jnp.concatenate(
            [picked[t * slots : (t + 1) * slots] * factor for t in range(steps)], axis=0
        )
        return total + jnp.dot(terms, reception[at, :], preferred_element_type=F32)

    for copy in copies[:3]:
        copy.wait()
    total = jnp.zeros((steps * slots, width), F32)
    for index in range(rays // chunk):
        total = history_part(index, total)
    hist_terms[...] = total

    def send_far(step):
        terms = hist_terms[pl.ds(step * slots, slots), :]
        if step > 0:
            picked = jnp.dot(
                new_pick[pl.ds(step * slots, slots), :], cur_all[...], preferred_element_type=F32
            ).astype(BF16)

            def new_part(index, total):
                at = columns(index)
                ray = jnp.dot(picked, projection[:, at], preferred_element_type=F32).astype(BF16)
                return total + jnp.dot(
                    ray * factors[:, at], reception[at, :], preferred_element_type=F32
                )

            for index in range(rays // chunk):
                terms = new_part(index, terms)
        high = terms.astype(BF16)
        low = (terms - high.astype(F32)).astype(BF16)
        far = jnp.dot(
            target_pick[...], jnp.concatenate([high, low], axis=0), preferred_element_type=F32
        )
        far_send[step] = far.astype(BF16).reshape(peers, boxes, width)
        for offset in range(1, peers):
            for turn_by in range(spread):
                far_copy(step, offset, turn_by).start()

    row = lax.broadcasted_iota(jnp.int32, (boxes, width), 0)

    for step in range(steps):
        send_far(step)
        if step == 0:
            copies[3].wait()

            def split(index, carry):
                whole = inverse_v[index].T
                high = whole.astype(BF16)
                low = (whole - high.astype(F32)).astype(BF16)
                inverse_cat[index] = jnp.concatenate([high, low], axis=0)
                return carry

            lax.fori_loop(0, boxes, split, 0)
            copies[4].wait()
            copies[5].wait()
        wait_window(step)

        pieces = []
        for lag in range(lags):
            at = lag_span + step - (piece * lags + lag + 1)
            table = jnp.concatenate([win[0, at], win[1, at], win[2, at]], axis=0).astype(BF16)
            gathered = jnp.dot(near_pick[...], table, preferred_element_type=F32).astype(BF16)
            for n in range(near):
                pieces.append(gathered[n * boxes : (n + 1) * boxes])
        sources = jnp.concatenate(pieces, axis=1)

        def near_part(index, total):
            if step > 0:
                value = jnp.dot(sources, near_t[index], preferred_element_type=F32)
                return total + jnp.where(row == index, value, 0.0)
            blocks = jnp.concatenate(
                [near_v[index, n, lag] for lag in range(lags) for n in range(near)], axis=1
            )
            value = lax.dot_general(sources, blocks, NT_DIMS, preferred_element_type=F32)
            return total + jnp.where(row == index, value, 0.0)

        field = jnp.zeros((boxes, width), F32)
        for index in range(boxes):
            field = near_part(index, field)
        part[step, piece] = field + far_send[step, box].astype(F32)
        for offset in range(1, spread):
            part_copy(step, offset).start()
        if step == 0:

            def turn(index, carry):
                for lag in range(lags):
                    for n in range(near):
                        start = (lag * near + n) * width
                        near_t[index, pl.ds(start, width), :] = near_v[index, n, lag].T
                return carry

            lax.fori_loop(0, boxes, turn, 0)
        for offset in range(1, peers):
            for turn_by in range(spread):
                far_copy(step, offset, turn_by).wait_recv()
        around = jnp.zeros((boxes, width), F32)
        for offset in range(1, peers):
            for other in range(spread):
                around = around + far_recv[step, offset, other].astype(F32)
        for offset in range(1, spread):
            part_copy(step, offset).wait_recv()
        total = around + part[step, 0]
        for other in range(1, spread):
            total = total + part[step, other]

        drive = incident[:, step, :] - total
        high = drive.astype(BF16)
        low = (drive - high.astype(F32)).astype(BF16)
        left = jnp.concatenate(
            [
                jnp.concatenate([high, high], axis=1),
                jnp.concatenate([low, jnp.zeros_like(low)], axis=1),
            ],
            axis=0,
        )

        def solve_part(index, total):
            value = jnp.dot(left, inverse_cat[index], preferred_element_type=F32)
            return total + jnp.where(row == index, value[:boxes] + value[boxes:], 0.0)

        current = jnp.zeros((boxes, width), F32)
        for index in range(boxes):
            current = solve_part(index, current)
        current = current.astype(BF16)
        out[:, pl.ds(step * width, width)] = current
        if step < steps - 1:
            cur_all[pl.ds(step * boxes, boxes), :] = current
            win[1, lag_span + step] = current.astype(F32)
            start_window(step + 1)

    for step in range(steps):
        wait_window_sent(step)
        for offset in range(1, peers):
            for turn_by in range(spread):
                far_copy(step, offset, turn_by).wait_send()
        for offset in range(1, spread):
            part_copy(step, offset).wait_send()


def body(
    history_currents,
    history_rays,
    incident,
    near_blocks,
    near_partners,
    self_inverse,
    projection,
    reception,
    translations,
    send_source,
    send_delay,
    send_target,
    send_class,
    slot_counts,
):
    boxes, hist_len, width = history_currents.shape
    rays = history_rays.shape[2]
    steps = incident.shape[1]
    near, lags = near_blocks.shape[1:3]
    peers, dirs, subs = (lax.axis_size(a) for a in ("box", "dir", "sub"))
    spread = dirs * subs
    lag_span = lags * spread
    slots = peers * send_source.shape[2]
    smem = pl.BlockSpec(memory_space=pltpu.SMEM)
    vmem = pl.BlockSpec(memory_space=pltpu.VMEM)
    hbm = pl.BlockSpec(memory_space=pl.ANY)
    dma = pltpu.SemaphoreType.DMA
    currents = pl.pallas_call(
        functools.partial(march, peers, dirs, subs),
        out_shape=jax.ShapeDtypeStruct((boxes, steps * width), BF16),
        in_specs=[smem] * 6 + [vmem] * 2 + [hbm] * 6,
        out_specs=vmem,
        scratch_shapes=[
            pltpu.VMEM((boxes * hist_len, rays), BF16),
            pltpu.VMEM(near_blocks.shape, BF16),
            pltpu.VMEM((boxes, lags * near * width, width), BF16),
            pltpu.VMEM(self_inverse.shape, F32),
            pltpu.VMEM(projection.shape, BF16),
            pltpu.VMEM(reception.shape, BF16),
            pltpu.VMEM(translations.shape, BF16),
            pltpu.VMEM((boxes, 2 * width, width), BF16),
            pltpu.VMEM((boxes, hist_len, width), F32),
            pltpu.VMEM((3, lag_span + steps, boxes, width), F32),
            pltpu.VMEM((steps * boxes, width), BF16),
            pltpu.VMEM((near * boxes, 3 * boxes), BF16),
            pltpu.VMEM((steps * slots, steps * boxes), BF16),
            pltpu.VMEM((peers * boxes, 2 * slots), BF16),
            pltpu.VMEM((slots, rays), BF16),
            pltpu.VMEM((steps * slots, width), F32),
            pltpu.VMEM((steps, peers, boxes, width), BF16),
            pltpu.VMEM((steps, peers, spread, boxes, width), BF16),
            pltpu.VMEM((steps, spread, boxes, width), F32),
            dma((6,)),
            dma((steps, 2)),
            dma((steps, 2)),
            dma((steps, peers * spread)),
            dma((steps, peers * spread)),
            dma((steps, spread)),
            dma((steps, spread)),
        ],
        compiler_params=pltpu.CompilerParams(
            collective_id=0, has_side_effects=True, vmem_limit_bytes=60 * 1024 * 1024
        ),
    )(
        send_source,
        send_delay,
        send_target,
        send_class,
        slot_counts,
        near_partners,
        history_currents,
        incident,
        history_rays.reshape(boxes * hist_len, rays),
        near_blocks,
        self_inverse,
        projection,
        reception,
        translations,
    )
    currents = currents.reshape(boxes, steps, width)
    new_rays = jnp.einsum("bts,sk->btk", currents, projection, preferred_element_type=F32)
    return currents, new_rays.astype(BF16)


def solution(mesh):
    return jax.shard_map(
        body,
        mesh=mesh,
        in_specs=(
            P(("groups", "box"), None, None),
            P(("groups", "box"), None, ("dir", "sub")),
            P(("groups", "box"), None, None),
            P("box", None, ("dir", "sub"), None, None),
            P("box", None),
            P("box", None, None),
            P(None, ("dir", "sub")),
            P(("dir", "sub"), None),
            P(None, ("dir", "sub")),
            P("box", None, None),
            P("box", None, None),
            P("box", None, None),
            P("box", None, None),
            P("box", None),
        ),
        out_specs=(P(("groups", "box"), None, None), P(("groups", "box"), None, ("dir", "sub"))),
        check_vma=False,
    )
```
